256 devices in a mesh: grp: 8 (over x_hi, y), tile: 32 (over x_lo, z, core).
Axes of the slice: x: 4 (x_hi: 2, x_lo: 2; x = x_hi * 2 + x_lo), y: 4, z: 8, core: 2. Of those that a mesh axis runs over, the one named last changes fastest.
Arguments:
- center: int32 [8], replicated, may hold values from 0 to 7, each once
- pair_occ: int32 [16, 2], P('grp'), may hold values from 0 to 7
- slab_map: int32 [16], replicated, may hold values from 0 to 1791
- eps_occ: float32 [8], replicated, may hold values from -2 to -0.5
- eps_vir: float32 [1792], replicated, may hold values from 0.2 to 3
- vvvo: bfloat16 [8, 16, 1792, 1792], P('grp', None, 'tile'), may hold values from -0.0034179688 to 0.0034179688
- hole_amps: bfloat16 [8, 16, 1792, 200], P('grp', None, 'tile'), may hold values from -0.009765625 to 0.009765625
- pair_amps: bfloat16 [16, 1792, 1792], P('grp', 'tile'), may hold values from -6 to 6
- pair_ints: bfloat16 [16, 1792, 200], P('grp', 'tile'), may hold values from -6 to 6
Outputs:
- energy_rows: float32 [16, 1792], P(None, 'tile')
- energy_total: float32 [], replicated
The draws below stay inside these ranges and needn't reach their ends.
Inputs may be any that keep to these rules, and one draw needn't show every extreme that they name: `center`: each of 0 to 7 appears once.
All inputs are finite; a program needn't handle non-finite values.
Results may differ from the reference program's by a relative error of at most 0.0003.
Values may be sent and summed in bfloat16 or wider, within the bound.
A program may use at most 128 MiB of HBM per device.

```python
import math
import jax
import jax.numpy as jnp
from jax import lax

V = 1792
O = 200
A = 16
OCC = 8
PAIRS = 16


def place_ends(values, own_key, smallest, top_value):
    dims = values.shape
    index_at = [jax.random.randint(jax.random.fold_in(own_key, axis), (), 0, dims[axis]) for axis in range(len(dims))]
    values = values.at[tuple(index_at)].set(smallest)
    longest = dims.index(max(dims))
    index_at[longest] = (index_at[longest] + 1) % dims[longest]
    return values.at[tuple(index_at)].set(top_value)


def level_of(own_key, dims, split, smallest, high):
    factor_of = 1.0
    for axis_at, parts in split:
        steps = jax.random.uniform(jax.random.fold_in(jax.random.fold_in(own_key, 6), axis_at), (parts,), jnp.float32, smallest / len(split), high / len(split))
        factor_of = factor_of * jnp.repeat(jnp.exp(steps), dims[axis_at] // parts).reshape((-1,) + (1,) * (len(dims) - 1 - axis_at))
    return factor_of


def centred(stream_key, dims, scale, reach, shards=(), dtype=jnp.bfloat16):
    values = jax.random.normal(stream_key, dims, jnp.float32) * scale
    if len(shards) > 0:
        values = level_of(stream_key, dims, shards, -0.22, 0.18) * values
    return jnp.clip(values, min=-reach, max=reach).astype(dtype)


def setup_inputs(seed: int = 0) -> dict:
    key_list = jax.random.split(jax.random.key(seed), 10)
    return {
        "center": jax.random.permutation(key_list[0], OCC).astype(jnp.int32),
        "pair_occ": place_ends(jax.random.randint(key_list[1], (PAIRS, 2), 0, OCC), jax.random.fold_in(key_list[1], 1), 0, OCC - 1).astype(jnp.int32),
        "slab_map": place_ends(jax.random.randint(key_list[2], (A,), 0, V), jax.random.fold_in(key_list[2], 1), 0, V - 1).astype(jnp.int32),
        "eps_occ": jnp.clip(jax.random.uniform(key_list[3], (OCC,), jnp.float32, -2.0, -0.5), -2.0, -0.5),
        "eps_vir": jnp.clip(jnp.exp(jax.random.uniform(key_list[4], (V,), jnp.float32, math.log(0.2), math.log(3.0))), 0.2, 3.0),
        "vvvo": centred(key_list[5], (OCC, A, V, V), (V * V) ** -0.5, 0.0034179688, ((0, 8), (2, 32))),
        "hole_amps": centred(key_list[6], (OCC, A, V, O), (O * V) ** -0.5, 0.009765625, ((0, 8), (2, 32))),
        "pair_amps": centred(key_list[7], (PAIRS, V, V), 1.0, 6.0, ((0, 8), (1, 32))),
        "pair_ints": centred(key_list[8], (PAIRS, V, O), 1.0, 6.0, ((0, 8), (1, 32))),
    }


def contract(left, right):
    return lax.dot_general(left, right, (((1,), (1,)), ((), ())), preferred_element_type=jnp.float32)


def reference(center, pair_occ, slab_map, eps_occ, eps_vir, vvvo, hole_amps, pair_amps, pair_ints):
    target = center[0]
    integral_rows = lax.dynamic_index_in_dim(vvvo, target, 0, keepdims=False).reshape(A * V, V)
    hole_rows = lax.dynamic_index_in_dim(hole_amps, target, 0, keepdims=False).reshape(A * V, O)
    slab_energy = eps_vir[slab_map]
    outer_denom = (-(slab_energy[:, None] + eps_vir[None, :])).reshape(-1)
    center_energy = eps_occ[target]
    running = jnp.zeros((A * V,), jnp.float32)
    for pair_slot in range(PAIRS):
        occ_total = center_energy + eps_occ[pair_occ[pair_slot, 0]] + eps_occ[pair_occ[pair_slot, 1]]
        triples = contract(integral_rows, pair_amps[pair_slot]) - contract(hole_rows, pair_ints[pair_slot])
        denominator = occ_total + outer_denom[:, None] - eps_vir[None, :]
        running = running + jnp.sum(triples * triples / denominator, axis=1)
    energy_rows = running.reshape(A, V)
    return energy_rows, jnp.sum(energy_rows)
```

```python
import functools

import jax
import jax.numpy as jnp
from jax import lax
from jax.experimental import pallas as pl
from jax.experimental.pallas import tpu as pltpu
from jax.sharding import PartitionSpec as P

MESH = pl.DeviceIdType.MESH
DEPTH = 2048
CHUNK = 16
STEPS_ROWS = 14
MOVES = ((1, 0), (-1, 0), (0, 1), (0, -1))
PARENT = (
    (1, 2, 0, 3), (2, 0, 1, 3), (2, 0, 1, 3), (2, 0, 1, 3),
    (3, 1, 0, 2), (0, 1, 2, 3), (2, 1, 3, 0), (2, 1, 3, 0),
    (3, 1, 0, 2), (0, 1, 2, 3), (0, 3, 2, 1), (2, 3, 0, 1),
    (3, 1, 0, 2), (1, 2, 0, 3), (1, 2, 0, 3), (2, 3, 0, 1),
)


def tree_tables():
    def step(node, move, sign):
        return ((node // 4 + sign * move[0]) % 4) * 4 + (node % 4 + sign * move[1]) % 4

    depth = [[0] * 16 for _ in range(4)]
    child = [[0] * 4 for _ in range(4)]
    for tree in range(4):
        for node in range(1, 16):
            entered = PARENT[node][tree]
            child[tree][entered] |= 1 << step(node, MOVES[entered], -1)
            at, hops = node, 0
            while at != 0:
                at, hops = step(at, MOVES[PARENT[at][tree]], -1), hops + 1
            depth[tree][node] = hops
    planes = [[sum(((depth[t][v] >> b) & 1) << v for v in range(16)) for b in range(3)] for t in range(4)]
    return planes, child, max(max(d) for d in depth)


DEPTH_BITS, CHILD_BITS, DEEPEST = tree_tables()
STEPS = STEPS_ROWS + DEEPEST
RING_STEPS = (2, 4, 6, 8, 10, 12, 14)
SLOT_READY = (1, 4, 4, 8, 8, 12, 12, 14)
UNITS_PER_STEP = 5


def unit_schedule():
    units = sorted((max(2 * i + 1 + DEEPEST, SLOT_READY[o]), i, o) for i in range(7) for o in range(8))
    starts, at = [], 0
    for step in range(STEPS):
        starts.append(at)
        taken = 0
        while at < len(units) and units[at][0] <= step and (taken < UNITS_PER_STEP or step == STEPS - 1):
            at, taken = at + 1, taken + 1
    starts.append(at)
    assert at == len(units)
    codes = [i * 8 + o for _, i, o in units]
    words = [sum(c << (6 * n) for n, c in enumerate(codes[w : w + 5])) for w in range(0, len(codes), 5)]
    return starts, words


STARTS, WORDS = unit_schedule()


def pick(values, index):
    result = jnp.int32(values[0])
    for at in range(1, len(values)):
        if values[at] != values[at - 1]:
            result = jnp.where(index >= at, jnp.int32(values[at]), result)
    return result


def bit(mask, index):
    return jnp.bitwise_and(lax.shift_right_logical(jnp.int32(mask), index), 1)


def device(x, y, z, core):
    return (lax.div(x, 2) * 4 + y, lax.rem(x, 2) * 16 + z * 2 + core)


def kernel(
    owner, amps, rows, outer, col, out,
    mbuf, nbuf, obuf, acc, part, got1, got2,
    m_recv, m_send, z_recv, z_send, c_recv, c_send, local_sem, r1_recv, r1_send, r2_recv, r2_send,
):
    grp, tile = lax.axis_index("grp"), lax.axis_index("tile")
    y, x = lax.rem(grp, 4), lax.div(grp, 4) * 2 + lax.div(tile, 16)
    x_lo, z, core = lax.div(tile, 16), lax.div(lax.rem(tile, 16), 2), lax.rem(tile, 2)
    plane_pos = x * 4 + y
    tile0 = tile
    is_owner = grp == owner

    barrier = pltpu.get_barrier_semaphore()

    def plane_peer(n):
        pos = lax.rem(plane_pos + n, 16)
        return pos, device(lax.div(pos, 4), lax.rem(pos, 4), z, core)

    def tile_peer(n):
        pos = lax.rem(tile0 + n, 32)
        return pos, (grp, pos)

    def greet(peer_of):
        def one(n, carry):
            pl.semaphore_signal(barrier, inc=1, device_id=peer_of(n)[1], device_id_type=MESH)
            return carry

        return one

    lax.fori_loop(1, 16, greet(plane_peer), 0)
    lax.fori_loop(1, 32, greet(tile_peer), 0)

    own_rows = pltpu.make_async_copy(rows, mbuf.at[:, x_lo], local_sem.at[0])
    own_amps = pltpu.make_async_copy(amps, nbuf.at[z, pl.ds(pl.multiple_of(core * 112, 16), 112)], local_sem.at[1])
    pl.when(is_owner)(own_rows.start)
    own_amps.start()

    for slot in range(8):
        nbuf[slot, 224:256, :] = jnp.zeros((32, DEPTH), jnp.bfloat16)
    acc[...] = jnp.zeros_like(acc)
    part[...] = jnp.zeros_like(part)
    for n in range(14):
        line = jnp.broadcast_to(outer[n : n + 1, :], (128, 128))
        obuf[n // 2, (n % 2) * 128 : (n % 2) * 128 + 128, :] = line.T

    pl.semaphore_wait(barrier, 15 + 31)

    ahead = (device(x, y, lax.rem(z + 1, 8), core), device(x, y, lax.rem(z + 7, 8), core))
    sibling = device(x, y, z, 1 - core)
    piece = ((0, 64), (64, 48))

    def slot_of(p, d):
        return lax.rem(z + (8 - d if p == 0 else d), 8)

    def slot_rows(slot, whose, c):
        first, size = (0, 112) if c is None else piece[c]
        return nbuf.at[slot, pl.ds(pl.multiple_of(whose * 112 + first, 16), size)]


    def ring_send(p, d, c):
        first, size = piece[c]
        here = slot_rows(slot_of(p, d - 1), core, c)
        source = amps.at[pl.ds(first, size)] if d == 1 else here
        return pltpu.make_async_remote_copy(
            source, here, z_send.at[p, d - 1, c], z_recv.at[p, d - 1, c], device_id=ahead[p], device_id_type=MESH
        )

    def ring_got(p, d, c):
        here = slot_rows(slot_of(p, d), core, c)
        return pltpu.make_async_remote_copy(
            here, here, z_send.at[p, d - 1, c], z_recv.at[p, d - 1, c], device_id=ahead[p], device_id_type=MESH
        )

    def order_of(p, d):
        return 7 if d == 4 else (0 if d == 0 else 2 * d - 1 + p)

    def share(p, d, c):
        order = order_of(p, d)
        here = slot_rows(slot_of(p, d), core, c)
        source = amps if d == 0 else here
        n = 0 if c is None else c
        return pltpu.make_async_remote_copy(
            source, here, c_send.at[order, n], c_recv.at[order, n], device_id=sibling, device_id_type=MESH
        )

    def shared(p, d, c):
        order = order_of(p, d)
        here = slot_rows(slot_of(p, d), 1 - core, c)
        n = 0 if c is None else c
        return pltpu.make_async_remote_copy(
            here, here, c_send.at[order, n], c_recv.at[order, n], device_id=sibling, device_id_type=MESH
        )

    def travels(p, d, c):
        return d <= 3 or (d == 4 and p == c)

    for c in range(2):
        for p in range(2):
            ring_send(p, 1, c).start()
    share(0, 0, None).start()

    next_to = (
        device(lax.rem(x + 1, 4), y, z, core),
        device(lax.rem(x + 3, 4), y, z, core),
        device(x, lax.rem(y + 1, 4), z, core),
        device(x, lax.rem(y + 3, 4), z, core),
    )
    root_y, root_x = owner % 4, (owner // 4) * 2
    place = [lax.rem(x + 4 - root_x - s, 4) * 4 + lax.rem(y + 4 - root_y, 4) for s in range(2)]
    depth = [
        [sum(bit(DEPTH_BITS[t][b], place[s]) * (1 << b) for b in range(3)) for t in range(4)] for s in range(2)
    ]
    child = [[[bit(CHILD_BITS[t][d], place[s]) == 1 for d in range(4)] for t in range(4)] for s in range(2)]

    pl.when(is_owner)(own_rows.wait)
    own_amps.wait()

    def row_events(step):
        for t in range(4):
            for s in range(2):
                k = step - depth[s][t]

                @pl.when((k >= 0) & (k < STEPS_ROWS))
                def _(s=s, t=t, k=k):
                    q = 4 * k + t
                    part_rows = pl.ds(pl.multiple_of(lax.rem(q, 8) * CHUNK, CHUNK), CHUNK)
                    here = mbuf.at[lax.div(q, 8), s, part_rows]

                    def copy(d):
                        return pltpu.make_async_remote_copy(
                            here, here, m_send.at[s, t, d], m_recv.at[s, t, k],
                            device_id=next_to[d], device_id_type=MESH,
                        )

                    pl.when(place[s] != 0)(copy(0).wait_recv)
                    for d in range(4):
                        pl.when(child[s][t][d])(copy(d).start)

    def ring_event(n):
        d, c = (n // 2 + 1, n % 2) if n < 6 else (4, None)
        for p in range(2):
            cc = p if c is None else c
            ring_got(p, d, cc).wait_recv()
            if d < 4 and travels(p, d + 1, cc):
                ring_send(p, d + 1, cc).start()
            share(p, d, cc).start()

    def slots_shared(d):
        if d == 0:
            shared(0, 0, None).wait_recv()
        else:
            for p in range(2):
                for c in range(2):
                    if travels(p, d, c):
                        shared(p, d, c).wait_recv()

    def unit(u, carry):
        word = pick(WORDS, lax.div(u, 5))
        code = jnp.bitwise_and(lax.shift_right_logical(word, 6 * lax.rem(u, 5)), 63)
        i, o = lax.div(code, 8), lax.rem(code, 8)
        hops = lax.div(o + 1, 2)
        slot = lax.rem(jnp.where(lax.rem(o, 2) == 1, z + 8 - hops, z + hops), 8)
        left = mbuf[i].reshape(256, DEPTH)
        w = lax.dot_general(left, nbuf[slot], (((1,), (1,)), ((), ())), preferred_element_type=jnp.float32)
        base = obuf[i]
        line = col[pl.ds(slot, 1), :]
        total = acc[i]
        for h in range(2):
            wh = w[:, 128 * h : 128 * h + 128]
            total = total + wh * wh / (base + line[:, 128 * h : 128 * h + 128])
        acc[i] = total
        return carry

    def one_step(step, carry):
        row_events(step)
        for n, when in enumerate(RING_STEPS):
            pl.when(step == when)(functools.partial(ring_event, n))
        for d in range(5):
            pl.when(step == SLOT_READY[order_of(0, d)])(functools.partial(slots_shared, d))
        lax.fori_loop(pick(STARTS, step), pick(STARTS, step + 1), unit, 0)
        return carry

    lax.fori_loop(0, STEPS, one_step, 0)

    for n in range(14):
        block = acc[n // 2, (n % 2) * 128 : (n % 2) * 128 + 128, :]
        part[n % 2, n // 2 : n // 2 + 1, :] = jnp.sum(block.T, axis=0, keepdims=True)

    def first_copy(n):
        pos, peer = plane_peer(n)
        return pltpu.make_async_remote_copy(
            part.at[lax.rem(lax.div(pos, 4), 2)], got1.at[plane_pos], r1_send.at[n], r1_recv.at[plane_pos],
            device_id=peer, device_id_type=MESH,
        )

    def first_got(n):
        pos, peer = plane_peer(n)
        return pltpu.make_async_remote_copy(
            part.at[0], got1.at[pos], r1_send.at[n], r1_recv.at[pos], device_id=peer, device_id_type=MESH
        )

    def second_copy(n):
        pos, peer = tile_peer(n)
        return pltpu.make_async_remote_copy(
            got2.at[tile0], got2.at[tile0], r2_send.at[n], r2_recv.at[tile0], device_id=peer, device_id_type=MESH
        )

    def second_got(n):
        pos, peer = tile_peer(n)
        return pltpu.make_async_remote_copy(
            got2.at[pos], got2.at[pos], r2_send.at[n], r2_recv.at[pos], device_id=peer, device_id_type=MESH
        )

    def each(count, act):
        def one(n, carry):
            act(n)
            return carry

        lax.fori_loop(1, count, one, 0)

    each(16, lambda n: first_copy(n).start())
    got1[plane_pos] = part[x_lo]
    each(16, lambda n: first_got(n).wait_recv())
    summed = got1[0]
    for n in range(1, 16):
        summed = summed + got1[n]
    got2[tile0] = summed
    out[0:8, :] = summed
    each(32, lambda n: second_copy(n).start())

    each(16, lambda n: first_copy(n).wait_send())
    for s in range(2):
        for t in range(4):
            for d in range(4):

                @pl.when(child[s][t][d])
                def _(s=s, t=t, d=d):
                    whole = nbuf.at[0, pl.ds(0, STEPS_ROWS * CHUNK)]
                    pltpu.make_async_copy(whole, whole, m_send.at[s, t, d]).wait()

    share(0, 0, None).wait_send()
    for d in range(1, 5):
        for p in range(2):
            for c in range(2):
                if travels(p, d, c):
                    ring_send(p, d, c).wait_send()
                    share(p, d, c).wait_send()

    each(32, lambda n: second_got(n).wait_recv())
    everything = got2[0]
    for n in range(1, 32):
        everything = everything + got2[n]
    across = jnp.sum(everything, axis=1, keepdims=True)
    out[8:16, :] = jnp.broadcast_to(jnp.sum(across, axis=0, keepdims=True), (8, 128))
    each(32, lambda n: second_copy(n).wait_send())


def triples(owner, amps, rows, outer, col):
    bf16, f32 = jnp.bfloat16, jnp.float32
    return pl.pallas_call(
        functools.partial(kernel, owner),
        out_shape=jax.ShapeDtypeStruct((16, 128), f32),
        in_specs=[
            pl.BlockSpec(memory_space=pl.ANY),
            pl.BlockSpec(memory_space=pl.ANY),
            pl.BlockSpec(memory_space=pltpu.VMEM),
            pl.BlockSpec(memory_space=pltpu.VMEM),
        ],
        out_specs=pl.BlockSpec(memory_space=pltpu.VMEM),
        scratch_shapes=[
            pltpu.VMEM((7, 2, 128, DEPTH), bf16),
            pltpu.VMEM((8, 256, DEPTH), bf16),
            pltpu.VMEM((7, 256, 128), f32),
            pltpu.VMEM((7, 256, 128), f32),
            pltpu.VMEM((2, 8, 128), f32),
            pltpu.VMEM((16, 8, 128), f32),
            pltpu.VMEM((32, 8, 128), f32),
            pltpu.SemaphoreType.DMA((2, 4, STEPS_ROWS)),
            pltpu.SemaphoreType.DMA((2, 4, 4)),
            pltpu.SemaphoreType.DMA((2, 4, 2)),
            pltpu.SemaphoreType.DMA((2, 4, 2)),
            pltpu.SemaphoreType.DMA((8, 2)),
            pltpu.SemaphoreType.DMA((8, 2)),
            pltpu.SemaphoreType.DMA((2,)),
            pltpu.SemaphoreType.DMA((16,)),
            pltpu.SemaphoreType.DMA((16,)),
            pltpu.SemaphoreType.DMA((32,)),
            pltpu.SemaphoreType.DMA((32,)),
        ],
        compiler_params=pltpu.CompilerParams(
            collective_id=owner, has_side_effects=True, vmem_limit_bytes=48 << 20
        ),
        name="triples",
    )(amps, rows, outer, col)


def shards(center, pair_occ, slab_map, eps_occ, eps_vir, vvvo, hole_amps, pair_amps, pair_ints):
    virt_all = eps_vir.shape[0]
    tile = lax.axis_index("tile")
    x_lo, zc = tile // 16, tile % 16

    fill = DEPTH - 1792 - 200
    rows = jnp.concatenate(
        [vvvo[0].reshape(896, 1792), -hole_amps[0].reshape(896, 200), jnp.zeros((896, fill), jnp.bfloat16)], axis=1
    ).reshape(7, 128, DEPTH)
    amps = jnp.concatenate(
        [pair_amps.reshape(112, 1792), pair_ints.reshape(112, 200), jnp.zeros((112, fill), jnp.bfloat16)], axis=1
    )

    slab_energy = jnp.sum(jnp.where(slab_map[:, None] == jnp.arange(virt_all)[None, :], eps_vir[None, :], 0.0), axis=1)
    tile_energy = lax.dynamic_index_in_dim(eps_vir.reshape(2, 16, 56), zc, 1, keepdims=False)
    outer = -(slab_energy[None, :, None] + tile_energy[:, None, :])
    outer = outer.reshape(2, 7, 128).transpose(1, 0, 2).reshape(14, 128)
    outer = jnp.pad(outer, ((0, 2), (0, 0)))

    occ_index = jnp.arange(eps_occ.shape[0])
    center_energy = jnp.sum(jnp.where(occ_index == center[0], eps_occ, 0.0))
    pair_energy = jnp.sum(jnp.where(pair_occ[:, :, None] == occ_index, eps_occ, 0.0), axis=2)
    occ_sums = center_energy + pair_energy[:, 0] + pair_energy[:, 1]
    mine = lax.dynamic_index_in_dim(eps_vir.reshape(2, 8, 2, 1, 56), x_lo, 0, keepdims=False)
    col = (occ_sums[None, None, :, None] - mine).reshape(8, 224)
    col = jnp.pad(col, ((0, 0), (0, 32)), constant_values=-1.0)

    out = lax.switch(center[0], [functools.partial(triples, n) for n in range(8)], amps, rows, outer, col)
    return out[0:7].reshape(16, 56), out[8, 0]


def solution(mesh):
    in_specs = (
        P(),
        P("grp", None),
        P(),
        P(),
        P(),
        P("grp", None, "tile", None),
        P("grp", None, "tile", None),
        P("grp", "tile", None),
        P("grp", "tile", None),
    )
    out_specs = (P(None, "tile"), P())
    return jax.shard_map(shards, mesh=mesh, in_specs=in_specs, out_specs=out_specs, check_vma=False)
```

```python
import functools

import jax
import jax.numpy as jnp
from jax import lax
from jax.experimental import pallas as pl
from jax.experimental.pallas import tpu as pltpu
from jax.sharding import PartitionSpec as P

MESH = pl.DeviceIdType.MESH
DEPTH = 2048
CHUNK = 32
STEPS_ROWS = 14
MOVES = ((1, 0), (-1, 0), (0, 1), (0, -1))
PARENT = (
    (1, 2, 0, 3), (2, 0, 1, 3), (2, 0, 1, 3), (2, 0, 1, 3),
    (3, 1, 0, 2), (0, 1, 2, 3), (2, 1, 3, 0), (2, 1, 3, 0),
    (3, 1, 0, 2), (0, 1, 2, 3), (0, 3, 2, 1), (2, 3, 0, 1),
    (3, 1, 0, 2), (1, 2, 0, 3), (1, 2, 0, 3), (2, 3, 0, 1),
)


def tree_tables():
    def step(node, move, sign):
        return ((node // 4 + sign * move[0]) % 4) * 4 + (node % 4 + sign * move[1]) % 4

    depth = [[0] * 16 for _ in range(4)]
    child = [[0] * 4 for _ in range(4)]
    for tree in range(4):
        for node in range(1, 16):
            entered = PARENT[node][tree]
            child[tree][entered] |= 1 << step(node, MOVES[entered], -1)
            at, hops = node, 0
            while at != 0:
                at, hops = step(at, MOVES[PARENT[at][tree]], -1), hops + 1
            depth[tree][node] = hops
    planes = [[sum(((depth[t][v] >> b) & 1) << v for v in range(16)) for b in range(3)] for t in range(4)]
    return planes, child, max(max(d) for d in depth)


DEPTH_BITS, CHILD_BITS, DEEPEST = tree_tables()
LAG = 4
BLOCK_CHUNKS = 128 // CHUNK
FIRST_BLOCK = BLOCK_CHUNKS - 1 + LAG * DEEPEST
HALF_STEPS = FIRST_BLOCK + 6 * BLOCK_CHUNKS + 1
RING_STEPS = (7, 11, 16, 20, 25, 29, 33)
PAIR_READY = (12, 21, 30, 35)
UNITS_A_STEP = 1


def unit_schedule():
    units = sorted((max(FIRST_BLOCK + BLOCK_CHUNKS * i, PAIR_READY[o]), i, o) for i in range(7) for o in range(4))
    counts, at = [], 0
    for step in range(HALF_STEPS - 1):
        ready = sum(when <= step for when, _, _ in units)
        counts.append(min(ready - at, UNITS_A_STEP))
        at += counts[-1]
    counts.append(len(units) - at)
    assert max(counts) < 16
    runs = [sum(c << (4 * n) for n, c in enumerate(counts[w : w + 7])) for w in range(0, HALF_STEPS, 7)]
    codes = [i * 4 + o for _, i, o in units]
    words = [sum(c << (5 * n) for n, c in enumerate(codes[w : w + 6])) for w in range(0, len(codes), 6)]
    return runs, words


RUNS, WORDS = unit_schedule()


def pick(values, index):
    result = jnp.int32(values[0])
    for at in range(1, len(values)):
        if values[at] != values[at - 1]:
            result = jnp.where(index >= at, jnp.int32(values[at]), result)
    return result


def bit(mask, index):
    return jnp.bitwise_and(lax.shift_right_logical(jnp.int32(mask), index), 1)


def device(x, y, z, core):
    return (lax.div(x, 2) * 4 + y, lax.rem(x, 2) * 16 + z * 2 + core)


def kernel(
    owner, center, pair_occ, slab_map, eps_occ, eps_vir, eps_tiles, vvvo, hole, amps, ints, out,
    mbuf, nbuf, obuf, acc, colabs, col, part, got1, got2,
    m_recv, m_send, z_recv, z_send, c_recv, c_send, local_sem, f_recv, f_send,
):
    grp, tile = lax.axis_index("grp"), lax.axis_index("tile")
    x_lo, z, core = lax.div(tile, 16), lax.div(lax.rem(tile, 16), 2), lax.rem(tile, 2)
    y, x = lax.rem(grp, 4), lax.div(grp, 4) * 2 + x_lo
    plane_pos, line_pos = x * 4 + y, z * 2 + core
    is_owner = grp == owner

    def plane_peer(n):
        pos = lax.rem(plane_pos + n, 16)
        return pos, device(lax.div(pos, 4), lax.rem(pos, 4), z, core)

    def line_peer(n):
        pos = lax.rem(line_pos + n, 16)
        return pos, device(x, y, lax.div(pos, 2), lax.rem(pos, 2))

    own_rows = pltpu.make_async_copy(vvvo, mbuf.at[:, x_lo, :, pl.ds(0, 1792)], local_sem.at[0])
    own_amps = pltpu.make_async_copy(
        amps, nbuf.at[0, pl.ds(pl.multiple_of(core * 112, 16), 112), pl.ds(0, 1792)], local_sem.at[1]
    )
    pl.when(is_owner)(own_rows.start)
    own_amps.start()

    barrier = pltpu.get_barrier_semaphore()
    for peer_of in (plane_peer, line_peer):
        for n in range(1, 16):
            pl.semaphore_signal(barrier, inc=1, device_id=peer_of(n)[1], device_id_type=MESH)

    zeros = jnp.zeros((112, 56), jnp.bfloat16)
    own_half = pl.ds(pl.multiple_of(core * 112, 16), 112)
    nbuf[0, own_half, 1792:2048] = jnp.concatenate([-ints[...], zeros], axis=1)

    @pl.when(is_owner)
    def _():
        for i in range(7):
            filled = jnp.concatenate([hole[i], jnp.zeros((128, 56), jnp.bfloat16)], axis=1)
            mbuf[i, x_lo, :, 1792:2048] = filled

    lane = lax.broadcasted_iota(jnp.int32, (8, 128), 1)
    flat = lax.broadcasted_iota(jnp.int32, (8, 128), 0) * 128 + lane
    slab = lax.shift_right_logical(flat * 1171, 16)
    within = flat - slab * 56
    slab_part = jnp.zeros((8, 128), jnp.float32)
    for a in range(16):
        slab_part = jnp.where(slab == a, eps_vir[slab_map[a]], slab_part)
    for s in range(2):
        tile_part = jnp.zeros((8, 128), jnp.float32)
        for r in range(56):
            tile_part = jnp.where(within == r, eps_vir[(s * 16 + z * 2 + core) * 56 + r], tile_part)
        outer = -(slab_part + tile_part)
        for i in range(7):
            line = jnp.broadcast_to(outer[i : i + 1, :], (128, 128))
            obuf[i, s * 128 : s * 128 + 128, :] = line.T
    occ = [eps_occ[center[0]] + eps_occ[pair_occ[p, 0]] + eps_occ[pair_occ[p, 1]] for p in range(2)]
    even = eps_tiles[pl.ds(x_lo * 16, 8, stride=2), :]
    odd = eps_tiles[pl.ds(x_lo * 16 + 1, 8, stride=2), :]
    colabs[:, 0:128] = jnp.where(
        lane < 56,
        occ[0] - even,
        jnp.where(lane < 112, occ[1] - pltpu.roll(even, 56, 1), occ[0] - pltpu.roll(odd, 112, 1)),
    )
    colabs[:, 128:256] = jnp.where(
        lane < 40,
        occ[0] - pltpu.roll(odd, 112, 1),
        jnp.where(lane < 96, occ[1] - pltpu.roll(odd, 40, 1), -1.0),
    )
    for o in range(8):
        hops = (o + 1) // 2
        at = lax.rem(z + (8 - hops if o % 2 == 1 else hops), 8)
        col[o : o + 1, :] = colabs[pl.ds(at, 1), :]

    for slot in range(8):
        nbuf[slot, 224:256, :] = jnp.zeros((32, DEPTH), jnp.bfloat16)
    acc[...] = jnp.zeros_like(acc)
    part[...] = jnp.zeros_like(part)

    ahead = (device(x, y, lax.rem(z + 1, 8), core), device(x, y, lax.rem(z + 7, 8), core))
    sibling = device(x, y, z, 1 - core)
    piece = ((0, 64), (64, 48))

    def order_of(p, d):
        return 7 if d == 4 else (0 if d == 0 else 2 * d - 1 + p)

    def slot_rows(p, d, whose, c):
        first, size = (0, 112) if c is None else piece[c]
        return nbuf.at[order_of(p, d), pl.ds(pl.multiple_of(whose * 112 + first, 16), size)]

    def ring(p, d, c):
        return pltpu.make_async_remote_copy(
            slot_rows(p, d - 1, core, c), slot_rows(p, d, core, c), z_send.at[p, d - 1, c], z_recv.at[p, d - 1, c],
            device_id=ahead[p], device_id_type=MESH,
        )

    def share(p, d, c):
        here = slot_rows(p, d, core, c)
        sems = order_of(p, d), 0 if c is None else c
        return pltpu.make_async_remote_copy(
            here, here, c_send.at[sems], c_recv.at[sems], device_id=sibling, device_id_type=MESH
        )

    def shared(p, d, c):
        here = slot_rows(p, d, 1 - core, c)
        sems = order_of(p, d), 0 if c is None else c
        return pltpu.make_async_remote_copy(
            here, here, c_send.at[sems], c_recv.at[sems], device_id=sibling, device_id_type=MESH
        )

    def travels(p, d, c):
        return d <= 3 or (d == 4 and p == c)

    next_to = (
        device(lax.rem(x + 1, 4), y, z, core),
        device(lax.rem(x + 3, 4), y, z, core),
        device(x, lax.rem(y + 1, 4), z, core),
        device(x, lax.rem(y + 3, 4), z, core),
    )
    root_y, root_x = owner % 4, (owner // 4) * 2
    place = [lax.rem(x + 4 - root_x - s, 4) * 4 + lax.rem(y + 4 - root_y, 4) for s in range(2)]

    def of_core(table, j):
        return jnp.where(core == 0, jnp.int32(table[j]), jnp.int32(table[j + 2]))

    first_half = [
        [
            s + LAG * sum(bit(of_core([DEPTH_BITS[t][b] for t in range(4)], j), place[s]) * (1 << b) for b in range(3))
            for j in range(2)
        ]
        for s in range(2)
    ]
    child = [
        [[bit(of_core([CHILD_BITS[t][d] for t in range(4)], j), place[s]) == 1 for d in range(4)] for j in range(2)]
        for s in range(2)
    ]

    passes = [[child[s][j][0] | child[s][j][1] | child[s][j][2] | child[s][j][3] for j in range(2)] for s in range(2)]

    own_amps.wait()
    pl.semaphore_wait(barrier, 15 + 15)
    for c in range(2):
        for p in range(2):
            ring(p, 1, c).start()
    share(0, 0, None).start()
    pl.when(is_owner)(own_rows.wait)

    def row_events(half):
        for s in range(2):
            for j in range(2):
                since = half - first_half[s][j]

                @pl.when(passes[s][j] & (since >= 0) & (since < 2 * STEPS_ROWS) & (jnp.bitwise_and(since, 1) == 0))
                def _(s=s, j=j, since=since):
                    k = lax.shift_right_logical(since, 1)
                    q = since + j
                    part_rows = pl.ds(pl.multiple_of(lax.rem(q, BLOCK_CHUNKS) * CHUNK, CHUNK), CHUNK)
                    here = mbuf.at[lax.div(q, BLOCK_CHUNKS), s, part_rows]

                    def copy(d):
                        return pltpu.make_async_remote_copy(
                            here, here, m_send.at[s, j, d], m_recv.at[s, j, k],
                            device_id=next_to[d], device_id_type=MESH,
                        )

                    pl.when(place[s] != 0)(copy(0).wait_recv)
                    for d in range(4):
                        pl.when(child[s][j][d])(copy(d).start)

    def last_chunks(i):
        for s in range(2):
            for j in range(2):

                @pl.when(jnp.logical_not(passes[s][j]))
                def _(s=s, j=j):
                    for n in range(BLOCK_CHUNKS // 2):
                        here = mbuf.at[i, s, pl.ds((2 * n + j) * CHUNK, CHUNK)]
                        pltpu.make_async_remote_copy(
                            here, here, m_send.at[s, j, 0], m_recv.at[s, j, BLOCK_CHUNKS // 2 * i + n],
                            device_id=next_to[0], device_id_type=MESH,
                        ).wait_recv()

    def ring_event(n):
        d, c = (n // 2 + 1, n % 2) if n < 6 else (4, None)
        for p in range(2):
            cc = p if c is None else c
            ring(p, d, cc).wait_recv()
            if d < 4 and travels(p, d + 1, cc):
                ring(p, d + 1, cc).start()
            share(p, d, cc).start()

    def slots_shared(d):
        if d == 1:
            shared(0, 0, None).wait_recv()
        for p in range(2):
            for c in range(2):
                if travels(p, d, c):
                    shared(p, d, c).wait_recv()

    def unit(u, carry):
        word = pick(WORDS, lax.div(u, 6))
        code = jnp.bitwise_and(lax.shift_right_logical(word, 5 * lax.rem(u, 6)), 31)
        i, o = lax.div(code, 4), lax.rem(code, 4) * 2
        left = mbuf[i].reshape(256, DEPTH)
        right = nbuf[pl.ds(o, 2)].reshape(512, DEPTH)
        w = lax.dot_general(left, right, (((1,), (1,)), ((), ())), preferred_element_type=jnp.float32)
        base = obuf[i]
        total = acc[i]
        for n in range(2):
            line = col[pl.ds(o + n, 1), :]
            for h in range(2):
                wh = w[:, 256 * n + 128 * h : 256 * n + 128 * h + 128]
                total = total + wh * wh / (base + line[:, 128 * h : 128 * h + 128])
        acc[i] = total

        @pl.when(o == 6)
        def _():
            for s in range(2):
                across = jnp.sum(total[128 * s : 128 * s + 128, :].T, axis=0, keepdims=True)
                part[s, pl.ds(i, 1), :] = across

        return carry

    def one_half(half, done):
        row_events(half)
        for n, when in enumerate(RING_STEPS):
            pl.when(half == when)(functools.partial(ring_event, n))
        for d in range(1, 5):
            pl.when(half == PAIR_READY[d - 1])(functools.partial(slots_shared, d))
        block = half - FIRST_BLOCK

        @pl.when((block >= 0) & (lax.rem(block, BLOCK_CHUNKS) == 0))
        def _():
            last_chunks(lax.div(block, BLOCK_CHUNKS))

        word = lax.div(half, 7)
        runs = jnp.bitwise_and(lax.shift_right_logical(pick(RUNS, word), 4 * (half - 7 * word)), 15)
        lax.fori_loop(done, done + runs, unit, 0)
        return done + runs

    lax.fori_loop(0, HALF_STEPS, one_half, jnp.int32(0))

    local = jnp.sum(part[0] + part[1], axis=0, keepdims=True)
    part[0, 7:8, :] = local
    part[1, 7:8, :] = local

    def exchange(stage, got, own_pos, peer_of, source):
        for n in range(1, 16):
            pos, peer = peer_of(n)
            pltpu.make_async_remote_copy(
                source(pos), got.at[own_pos], f_send.at[stage], f_recv.at[stage], device_id=peer, device_id_type=MESH
            ).start()

    def settle(stage, got, sems):
        whole = got.at[pl.ds(0, 15)]
        pltpu.make_async_copy(whole, whole, sems.at[stage]).wait()

    exchange(0, got1, plane_pos, plane_peer, lambda pos: part.at[lax.rem(lax.div(pos, 4), 2)])
    got1[plane_pos] = part[x_lo]

    for s in range(2):
        for j in range(2):
            for d in range(4):

                @pl.when(child[s][j][d])
                def _(s=s, j=j, d=d):
                    whole = mbuf.at[:, 0, pl.ds(0, STEPS_ROWS * CHUNK // 7)]
                    pltpu.make_async_copy(whole, whole, m_send.at[s, j, d]).wait()

    share(0, 0, None).wait_send()
    for d in range(1, 5):
        for p in range(2):
            for c in range(2):
                if travels(p, d, c):
                    ring(p, d, c).wait_send()
                    share(p, d, c).wait_send()

    settle(0, got1, f_recv)
    rows = got1[0]
    for n in range(1, 16):
        rows = rows + got1[n]
    got2[line_pos] = rows
    exchange(1, got2, line_pos, line_peer, lambda pos: got2.at[line_pos])
    out[0:8, :] = rows
    settle(0, got1, f_send)
    settle(1, got2, f_recv)
    every = got2[0]
    for n in range(1, 16):
        every = every + got2[n]
    out[8:16, :] = jnp.broadcast_to(jnp.sum(every[7:8, :], axis=1, keepdims=True), (8, 128))
    settle(1, got2, f_send)


def triples(owner, *operands):
    bf16, f32 = jnp.bfloat16, jnp.float32
    smem, vmem = pl.BlockSpec(memory_space=pltpu.SMEM), pl.BlockSpec(memory_space=pltpu.VMEM)
    anywhere = pl.BlockSpec(memory_space=pl.ANY)
    return pl.pallas_call(
        functools.partial(kernel, owner),
        out_shape=jax.ShapeDtypeStruct((16, 128), f32),
        in_specs=[smem, smem, smem, smem, smem, vmem, anywhere, vmem, anywhere, vmem],
        out_specs=vmem,
        scratch_shapes=[
            pltpu.VMEM((7, 2, 128, DEPTH), bf16),
            pltpu.VMEM((8, 256, DEPTH), bf16),
            pltpu.VMEM((7, 256, 128), f32),
            pltpu.VMEM((7, 256, 128), f32),
            pltpu.VMEM((8, 256), f32),
            pltpu.VMEM((8, 256), f32),
            pltpu.VMEM((2, 8, 128), f32),
            pltpu.VMEM((16, 8, 128), f32),
            pltpu.VMEM((16, 8, 128), f32),
            pltpu.SemaphoreType.DMA((2, 2, STEPS_ROWS)),
            pltpu.SemaphoreType.DMA((2, 2, 4)),
            pltpu.SemaphoreType.DMA((2, 4, 2)),
            pltpu.SemaphoreType.DMA((2, 4, 2)),
            pltpu.SemaphoreType.DMA((8, 2)),
            pltpu.SemaphoreType.DMA((8, 2)),
            pltpu.SemaphoreType.DMA((2,)),
            pltpu.SemaphoreType.DMA((2,)),
            pltpu.SemaphoreType.DMA((2,)),
        ],
        compiler_params=pltpu.CompilerParams(
            collective_id=owner, has_side_effects=True, vmem_limit_bytes=48 << 20
        ),
        name="triples",
    )(*operands)


def shards(center, pair_occ, slab_map, eps_occ, eps_vir, vvvo, hole_amps, pair_amps, pair_ints):
    operands = (
        center,
        pair_occ,
        slab_map,
        eps_occ,
        eps_vir,
        jnp.pad(eps_vir.reshape(32, 56), ((0, 0), (0, 72))),
        vvvo.reshape(7, 128, 1792),
        hole_amps.reshape(7, 128, 200),
        pair_amps.reshape(112, 1792),
        pair_ints.reshape(112, 200),
    )
    out = lax.switch(center[0], [functools.partial(triples, n) for n in range(8)], *operands)
    return out[0:7].reshape(16, 56), out[8, 0]


def solution(mesh):
    in_specs = (
        P(),
        P("grp", None),
        P(),
        P(),
        P(),
        P("grp", None, "tile", None),
        P("grp", None, "tile", None),
        P("grp", "tile", None),
        P("grp", "tile", None),
    )
    out_specs = (P(None, "tile"), P())
    return jax.shard_map(shards, mesh=mesh, in_specs=in_specs, out_specs=out_specs, check_vma=False)
```

```python
import functools

import jax
import jax.numpy as jnp
from jax import lax
from jax.experimental import pallas as pl
from jax.experimental.pallas import tpu as pltpu
from jax.sharding import PartitionSpec as P

MESH = pl.DeviceIdType.MESH
DEPTH = 2048
CHUNK = 32
STEPS_ROWS = 14
MOVES = ((1, 0), (-1, 0), (0, 1), (0, -1))
PARENT = (
    (1, 2, 0, 3), (2, 0, 1, 3), (2, 0, 1, 3), (2, 0, 1, 3),
    (3, 1, 0, 2), (0, 1, 2, 3), (2, 1, 3, 0), (2, 1, 3, 0),
    (3, 1, 0, 2), (0, 1, 2, 3), (0, 3, 2, 1), (2, 3, 0, 1),
    (3, 1, 0, 2), (1, 2, 0, 3), (1, 2, 0, 3), (2, 3, 0, 1),
)


def tree_tables():
    def step(node, move, sign):
        return ((node // 4 + sign * move[0]) % 4) * 4 + (node % 4 + sign * move[1]) % 4

    depth = [[0] * 16 for _ in range(4)]
    child = [[0] * 4 for _ in range(4)]
    for tree in range(4):
        for node in range(1, 16):
            entered = PARENT[node][tree]
            child[tree][entered] |= 1 << step(node, MOVES[entered], -1)
            at, hops = node, 0
            while at != 0:
                at, hops = step(at, MOVES[PARENT[at][tree]], -1), hops + 1
            depth[tree][node] = hops
    planes = [[sum(((depth[t][v] >> b) & 1) << v for v in range(16)) for b in range(3)] for t in range(4)]
    return planes, child, max(max(d) for d in depth)


DEPTH_BITS, CHILD_BITS, DEEPEST = tree_tables()
LAG = 4
BLOCK_CHUNKS = 128 // CHUNK
FIRST_BLOCK = BLOCK_CHUNKS - 1 + LAG * DEEPEST
HALF_STEPS = FIRST_BLOCK + 6 * BLOCK_CHUNKS + 1
RING_STEPS = (7, 11, 15, 19, 24, 28, 31)
PAIR_READY = (12, 20, 29, 33)
UNITS_A_STEP = 2


def unit_schedule():
    units = sorted((max(FIRST_BLOCK + BLOCK_CHUNKS * i, PAIR_READY[2 * o + 1]), i, o) for i in range(7) for o in range(2))
    counts, at = [], 0
    for step in range(HALF_STEPS - 1):
        ready = sum(when <= step for when, _, _ in units)
        counts.append(min(ready - at, UNITS_A_STEP))
        at += counts[-1]
    counts.append(len(units) - at)
    assert max(counts) < 16
    runs = [sum(c << (4 * n) for n, c in enumerate(counts[w : w + 7])) for w in range(0, HALF_STEPS, 7)]
    codes = [i * 2 + o for _, i, o in units]
    words = [sum(c << (5 * n) for n, c in enumerate(codes[w : w + 6])) for w in range(0, len(codes), 6)]
    return runs, words


RUNS, WORDS = unit_schedule()


def pick(values, index):
    result = jnp.int32(values[0])
    for at in range(1, len(values)):
        if values[at] != values[at - 1]:
            result = jnp.where(index >= at, jnp.int32(values[at]), result)
    return result


def bit(mask, index):
    return jnp.bitwise_and(lax.shift_right_logical(jnp.int32(mask), index), 1)


def device(x, y, z, core):
    return (lax.div(x, 2) * 4 + y, lax.rem(x, 2) * 16 + z * 2 + core)


def kernel(
    owner, center, pair_occ, slab_map, eps_occ, eps_vir, eps_lines, vvvo, hole, amps, ints, out,
    mbuf, nbuf, obuf, acc, tiles, colabs, col, part, got1, got2,
    m_recv, m_send, z_recv, z_send, c_recv, c_send, local_sem, f_recv, f_send,
):
    grp, tile = lax.axis_index("grp"), lax.axis_index("tile")
    x_lo, z, core = lax.div(tile, 16), lax.div(lax.rem(tile, 16), 2), lax.rem(tile, 2)
    y, x = lax.rem(grp, 4), lax.div(grp, 4) * 2 + x_lo
    plane_pos, line_pos = x * 4 + y, z * 2 + core
    is_owner = grp == owner

    def plane_peer(n):
        pos = lax.rem(plane_pos + n, 16)
        return pos, device(lax.div(pos, 4), lax.rem(pos, 4), z, core)

    def line_peer(n):
        pos = lax.rem(line_pos + n, 16)
        return pos, device(x, y, lax.div(pos, 2), lax.rem(pos, 2))

    own_rows = pltpu.make_async_copy(vvvo, mbuf.at[:, x_lo, :, pl.ds(0, 1792)], local_sem.at[0])
    own_amps = pltpu.make_async_copy(
        amps, nbuf.at[0, pl.ds(pl.multiple_of(core * 112, 16), 112), pl.ds(0, 1792)], local_sem.at[1]
    )
    pl.when(is_owner)(own_rows.start)
    own_amps.start()

    barrier = pltpu.get_barrier_semaphore()
    for peer_of in (plane_peer, line_peer):
        for n in range(1, 16):
            pl.semaphore_signal(barrier, inc=1, device_id=peer_of(n)[1], device_id_type=MESH)

    zeros = jnp.zeros((112, 56), jnp.bfloat16)
    own_half = pl.ds(pl.multiple_of(core * 112, 16), 112)
    nbuf[0, own_half, 1792:2048] = jnp.concatenate([-ints[...], zeros], axis=1)

    @pl.when(is_owner)
    def _():
        for i in range(7):
            filled = jnp.concatenate([hole[i], jnp.zeros((128, 56), jnp.bfloat16)], axis=1)
            mbuf[i, x_lo, :, 1792:2048] = filled

    lane = lax.broadcasted_iota(jnp.int32, (8, 128), 1)
    flat = lax.broadcasted_iota(jnp.int32, (8, 128), 0) * 128 + lane
    slab = lax.shift_right_logical(flat * 1171, 16)
    within = flat - slab * 56
    slab_part = jnp.zeros((8, 128), jnp.float32)
    for a in range(16):
        slab_part = jnp.where(slab == a, eps_vir[slab_map[a]], slab_part)
    for s in range(2):
        tile_part = jnp.zeros((8, 128), jnp.float32)
        for r in range(56):
            tile_part = jnp.where(within == r, eps_vir[(s * 16 + z * 2 + core) * 56 + r], tile_part)
        outer = -(slab_part + tile_part)
        for i in range(7):
            line = jnp.broadcast_to(outer[i : i + 1, :], (128, 128))
            obuf[i, s * 128 : s * 128 + 128, :] = line.T
    occ = [eps_occ[center[0]] + eps_occ[pair_occ[p, 0]] + eps_occ[pair_occ[p, 1]] for p in range(2)]
    for n in range(16):
        first = (x_lo * 16 + n) * 56
        line, off = lax.div(first, 128), lax.rem(first, 128)
        both = [
            jnp.broadcast_to(eps_lines[pl.ds(lax.min(line + more, 13), 1), :], (8, 128)) for more in range(2)
        ]
        turned = [pltpu.roll(part_of, lax.rem(128 - off, 128), 1) for part_of in both]
        here = jnp.where(lane + off < 128, turned[0], turned[1])
        tiles[n % 2, n // 2 : n // 2 + 1, :] = here[0:1, :]
    even, odd = tiles[0], tiles[1]
    colabs[:, 0:128] = jnp.where(
        lane < 56,
        occ[0] - even,
        jnp.where(lane < 112, occ[1] - pltpu.roll(even, 56, 1), occ[0] - pltpu.roll(odd, 112, 1)),
    )
    colabs[:, 128:256] = jnp.where(
        lane < 40,
        occ[0] - pltpu.roll(odd, 112, 1),
        jnp.where(lane < 96, occ[1] - pltpu.roll(odd, 40, 1), -1.0),
    )
    for o in range(8):
        hops = (o + 1) // 2
        at = lax.rem(z + (8 - hops if o % 2 == 1 else hops), 8)
        col[o : o + 1, :] = colabs[pl.ds(at, 1), :]

    for slot in range(8):
        nbuf[slot, 224:256, :] = jnp.zeros((32, DEPTH), jnp.bfloat16)
    acc[...] = jnp.zeros_like(acc)
    part[...] = jnp.zeros_like(part)

    ahead = (device(x, y, lax.rem(z + 1, 8), core), device(x, y, lax.rem(z + 7, 8), core))
    sibling = device(x, y, z, 1 - core)
    piece = ((0, 64), (64, 48))

    def order_of(p, d):
        return 7 if d == 4 else (0 if d == 0 else 2 * d - 1 + p)

    def slot_rows(p, d, whose, c):
        first, size = (0, 112) if c is None else piece[c]
        return nbuf.at[order_of(p, d), pl.ds(pl.multiple_of(whose * 112 + first, 16), size)]

    def ring(p, d, c):
        return pltpu.make_async_remote_copy(
            slot_rows(p, d - 1, core, c), slot_rows(p, d, core, c), z_send.at[p, d - 1, c], z_recv.at[p, d - 1, c],
            device_id=ahead[p], device_id_type=MESH,
        )

    def share(p, d, c):
        here = slot_rows(p, d, core, c)
        sems = order_of(p, d), 0 if c is None else c
        return pltpu.make_async_remote_copy(
            here, here, c_send.at[sems], c_recv.at[sems], device_id=sibling, device_id_type=MESH
        )

    def shared(p, d, c):
        here = slot_rows(p, d, 1 - core, c)
        sems = order_of(p, d), 0 if c is None else c
        return pltpu.make_async_remote_copy(
            here, here, c_send.at[sems], c_recv.at[sems], device_id=sibling, device_id_type=MESH
        )

    def travels(p, d, c):
        return d <= 3 or (d == 4 and p == c)

    next_to = (
        device(lax.rem(x + 1, 4), y, z, core),
        device(lax.rem(x + 3, 4), y, z, core),
        device(x, lax.rem(y + 1, 4), z, core),
        device(x, lax.rem(y + 3, 4), z, core),
    )
    root_y, root_x = owner % 4, (owner // 4) * 2
    place = [lax.rem(x + 4 - root_x - s, 4) * 4 + lax.rem(y + 4 - root_y, 4) for s in range(2)]

    def of_core(table, j):
        return jnp.where(core == 0, jnp.int32(table[j]), jnp.int32(table[j + 2]))

    first_half = [
        [
            s + LAG * sum(bit(of_core([DEPTH_BITS[t][b] for t in range(4)], j), place[s]) * (1 << b) for b in range(3))
            for j in range(2)
        ]
        for s in range(2)
    ]
    child = [
        [[bit(of_core([CHILD_BITS[t][d] for t in range(4)], j), place[s]) == 1 for d in range(4)] for j in range(2)]
        for s in range(2)
    ]

    passes = [[child[s][j][0] | child[s][j][1] | child[s][j][2] | child[s][j][3] for j in range(2)] for s in range(2)]

    own_amps.wait()
    pl.semaphore_wait(barrier, 15 + 15)
    for c in range(2):
        for p in range(2):
            ring(p, 1, c).start()
    share(0, 0, None).start()
    pl.when(is_owner)(own_rows.wait)

    def row_events(half):
        for s in range(2):
            for j in range(2):
                since = half - first_half[s][j]

                @pl.when(passes[s][j] & (since >= 0) & (since < 2 * STEPS_ROWS) & (jnp.bitwise_and(since, 1) == 0))
                def _(s=s, j=j, since=since):
                    k = lax.shift_right_logical(since, 1)
                    q = since + j
                    part_rows = pl.ds(pl.multiple_of(lax.rem(q, BLOCK_CHUNKS) * CHUNK, CHUNK), CHUNK)
                    here = mbuf.at[lax.div(q, BLOCK_CHUNKS), s, part_rows]

                    def copy(d):
                        return pltpu.make_async_remote_copy(
                            here, here, m_send.at[s, j, d], m_recv.at[s, j, k],
                            device_id=next_to[d], device_id_type=MESH,
                        )

                    pl.when(place[s] != 0)(copy(0).wait_recv)
                    for d in range(4):
                        pl.when(child[s][j][d])(copy(d).start)

    def last_chunks(i):
        for s in range(2):
            for j in range(2):

                @pl.when(jnp.logical_not(passes[s][j]))
                def _(s=s, j=j):
                    for n in range(BLOCK_CHUNKS // 2):
                        here = mbuf.at[i, s, pl.ds((2 * n + j) * CHUNK, CHUNK)]
                        pltpu.make_async_remote_copy(
                            here, here, m_send.at[s, j, 0], m_recv.at[s, j, BLOCK_CHUNKS // 2 * i + n],
                            device_id=next_to[0], device_id_type=MESH,
                        ).wait_recv()

    def ring_event(n):
        d, c = (n // 2 + 1, n % 2) if n < 6 else (4, None)
        for p in range(2):
            cc = p if c is None else c
            ring(p, d, cc).wait_recv()
            if d < 4 and travels(p, d + 1, cc):
                ring(p, d + 1, cc).start()
            share(p, d, cc).start()

    def slots_shared(d):
        if d == 1:
            shared(0, 0, None).wait_recv()
        for p in range(2):
            for c in range(2):
                if travels(p, d, c):
                    shared(p, d, c).wait_recv()

    def unit(u, carry):
        word = pick(WORDS, lax.div(u, 6))
        code = jnp.bitwise_and(lax.shift_right_logical(word, 5 * lax.rem(u, 6)), 31)
        i, o = lax.div(code, 2), lax.rem(code, 2) * 4
        left = mbuf[i].reshape(256, DEPTH)
        right = nbuf[pl.ds(o, 4)].reshape(1024, DEPTH)
        w = lax.dot_general(left, right, (((1,), (1,)), ((), ())), preferred_element_type=jnp.float32)
        base = obuf[i]
        total = acc[i]
        for n in range(4):
            line = col[pl.ds(o + n, 1), :]
            for h in range(2):
                wh = w[:, 256 * n + 128 * h : 256 * n + 128 * h + 128]
                total = total + wh * wh / (base + line[:, 128 * h : 128 * h + 128])
        acc[i] = total

        @pl.when(o == 4)
        def _():
            for s in range(2):
                across = jnp.sum(total[128 * s : 128 * s + 128, :].T, axis=0, keepdims=True)
                part[s, pl.ds(i, 1), :] = across

        return carry

    def one_half(half, done):
        row_events(half)
        for n, when in enumerate(RING_STEPS):
            pl.when(half == when)(functools.partial(ring_event, n))
        for d in range(1, 5):
            pl.when(half == PAIR_READY[d - 1])(functools.partial(slots_shared, d))
        block = half - FIRST_BLOCK

        @pl.when((block >= 0) & (lax.rem(block, BLOCK_CHUNKS) == 0))
        def _():
            last_chunks(lax.div(block, BLOCK_CHUNKS))

        word = lax.div(half, 7)
        runs = jnp.bitwise_and(lax.shift_right_logical(pick(RUNS, word), 4 * (half - 7 * word)), 15)
        lax.fori_loop(done, done + runs, unit, 0)
        return done + runs

    lax.fori_loop(0, HALF_STEPS, one_half, jnp.int32(0))

    local = jnp.sum(part[0] + part[1], axis=0, keepdims=True)
    part[0, 7:8, :] = local
    part[1, 7:8, :] = local

    def exchange(stage, got, own_pos, peer_of, source):
        for n in range(1, 16):
            pos, peer = peer_of(n)
            pltpu.make_async_remote_copy(
                source(pos), got.at[own_pos], f_send.at[stage], f_recv.at[stage], device_id=peer, device_id_type=MESH
            ).start()

    def settle(stage, got, sems):
        whole = got.at[pl.ds(0, 15)]
        pltpu.make_async_copy(whole, whole, sems.at[stage]).wait()

    exchange(0, got1, plane_pos, plane_peer, lambda pos: part.at[lax.rem(lax.div(pos, 4), 2)])
    got1[plane_pos] = part[x_lo]

    for s in range(2):
        for j in range(2):
            for d in range(4):

                @pl.when(child[s][j][d])
                def _(s=s, j=j, d=d):
                    whole = mbuf.at[:, 0, pl.ds(0, STEPS_ROWS * CHUNK // 7)]
                    pltpu.make_async_copy(whole, whole, m_send.at[s, j, d]).wait()

    share(0, 0, None).wait_send()
    for d in range(1, 5):
        for p in range(2):
            for c in range(2):
                if travels(p, d, c):
                    ring(p, d, c).wait_send()
                    share(p, d, c).wait_send()

    settle(0, got1, f_recv)
    rows = got1[0]
    for n in range(1, 16):
        rows = rows + got1[n]
    got2[line_pos] = rows
    exchange(1, got2, line_pos, line_peer, lambda pos: got2.at[line_pos])
    out[0:8, :] = rows
    settle(0, got1, f_send)
    settle(1, got2, f_recv)
    every = got2[0]
    for n in range(1, 16):
        every = every + got2[n]
    out[8:16, :] = jnp.broadcast_to(jnp.sum(every[7:8, :], axis=1, keepdims=True), (8, 128))
    settle(1, got2, f_send)


def triples(owner, *operands):
    bf16, f32 = jnp.bfloat16, jnp.float32
    smem, vmem = pl.BlockSpec(memory_space=pltpu.SMEM), pl.BlockSpec(memory_space=pltpu.VMEM)
    anywhere = pl.BlockSpec(memory_space=pl.ANY)
    return pl.pallas_call(
        functools.partial(kernel, owner),
        out_shape=jax.ShapeDtypeStruct((16, 128), f32),
        in_specs=[smem, smem, smem, smem, smem, vmem, anywhere, vmem, anywhere, vmem],
        out_specs=vmem,
        scratch_shapes=[
            pltpu.VMEM((7, 2, 128, DEPTH), bf16),
            pltpu.VMEM((8, 256, DEPTH), bf16),
            pltpu.VMEM((7, 256, 128), f32),
            pltpu.VMEM((7, 256, 128), f32),
            pltpu.VMEM((2, 8, 128), f32),
            pltpu.VMEM((8, 256), f32),
            pltpu.VMEM((8, 256), f32),
            pltpu.VMEM((2, 8, 128), f32),
            pltpu.VMEM((16, 8, 128), f32),
            pltpu.VMEM((16, 8, 128), f32),
            pltpu.SemaphoreType.DMA((2, 2, STEPS_ROWS)),
            pltpu.SemaphoreType.DMA((2, 2, 4)),
            pltpu.SemaphoreType.DMA((2, 4, 2)),
            pltpu.SemaphoreType.DMA((2, 4, 2)),
            pltpu.SemaphoreType.DMA((8, 2)),
            pltpu.SemaphoreType.DMA((8, 2)),
            pltpu.SemaphoreType.DMA((2,)),
            pltpu.SemaphoreType.DMA((2,)),
            pltpu.SemaphoreType.DMA((2,)),
        ],
        compiler_params=pltpu.CompilerParams(
            collective_id=owner, has_side_effects=True, vmem_limit_bytes=48 << 20
        ),
        name="triples",
    )(*operands)


def shards(center, pair_occ, slab_map, eps_occ, eps_vir, vvvo, hole_amps, pair_amps, pair_ints):
    operands = (
        center,
        pair_occ,
        slab_map,
        eps_occ,
        eps_vir,
        eps_vir.reshape(14, 128),
        vvvo.reshape(7, 128, 1792),
        hole_amps.reshape(7, 128, 200),
        pair_amps.reshape(112, 1792),
        pair_ints.reshape(112, 200),
    )
    out = lax.switch(center[0], [functools.partial(triples, n) for n in range(8)], *operands)
    return out[0:7].reshape(16, 56), out[8, 0]


def solution(mesh):
    in_specs = (
        P(),
        P("grp", None),
        P(),
        P(),
        P(),
        P("grp", None, "tile", None),
        P("grp", None, "tile", None),
        P("grp", "tile", None),
        P("grp", "tile", None),
    )
    out_specs = (P(None, "tile"), P())
    return jax.shard_map(shards, mesh=mesh, in_specs=in_specs, out_specs=out_specs, check_vma=False)
```

```python
import functools

import jax
import jax.numpy as jnp
from jax import lax
from jax.experimental import pallas as pl
from jax.experimental.pallas import tpu as pltpu
from jax.sharding import PartitionSpec as P

MESH = pl.DeviceIdType.MESH
DEPTH = 2048
CHUNK = 32
STEPS_ROWS = 14
MOVES = ((1, 0), (-1, 0), (0, 1), (0, -1))
PARENT = (
    (1, 2, 0, 3), (2, 0, 1, 3), (2, 0, 1, 3), (2, 0, 1, 3),
    (3, 1, 0, 2), (0, 1, 2, 3), (2, 1, 3, 0), (2, 1, 3, 0),
    (3, 1, 0, 2), (0, 1, 2, 3), (0, 3, 2, 1), (2, 3, 0, 1),
    (3, 1, 0, 2), (1, 2, 0, 3), (1, 2, 0, 3), (2, 3, 0, 1),
)


def tree_tables():
    def step(node, move, sign):
        return ((node // 4 + sign * move[0]) % 4) * 4 + (node % 4 + sign * move[1]) % 4

    depth = [[0] * 16 for _ in range(4)]
    child = [[0] * 4 for _ in range(4)]
    for tree in range(4):
        for node in range(1, 16):
            entered = PARENT[node][tree]
            child[tree][entered] |= 1 << step(node, MOVES[entered], -1)
            at, hops = node, 0
            while at != 0:
                at, hops = step(at, MOVES[PARENT[at][tree]], -1), hops + 1
            depth[tree][node] = hops
    planes = [[sum(((depth[t][v] >> b) & 1) << v for v in range(16)) for b in range(3)] for t in range(4)]
    return planes, child, max(max(d) for d in depth)


DEPTH_BITS, CHILD_BITS, DEEPEST = tree_tables()
LAG = 4
BLOCK_CHUNKS = 128 // CHUNK
FIRST_BLOCK = BLOCK_CHUNKS - 1 + LAG * DEEPEST
HALF_STEPS = FIRST_BLOCK + 6 * BLOCK_CHUNKS + 1
RING_STEPS = (7, 10, 14, 17, 21, 25, 28)
PAIR_READY = (12, 19, 27, 31)
UNITS_A_STEP = 1


def unit_schedule():
    units = sorted((max(FIRST_BLOCK + BLOCK_CHUNKS * i, PAIR_READY[2 * o + 1]), i, o) for i in range(7) for o in range(2))
    counts, at = [], 0
    for step in range(HALF_STEPS - 1):
        ready = sum(when <= step for when, _, _ in units)
        counts.append(min(ready - at, UNITS_A_STEP))
        at += counts[-1]
    counts.append(len(units) - at)
    assert max(counts) < 16
    runs = [sum(c << (4 * n) for n, c in enumerate(counts[w : w + 7])) for w in range(0, HALF_STEPS, 7)]
    codes = [i * 2 + o for _, i, o in units]
    words = [sum(c << (5 * n) for n, c in enumerate(codes[w : w + 6])) for w in range(0, len(codes), 6)]
    return runs, words


RUNS, WORDS = unit_schedule()


def pick(values, index):
    result = jnp.int32(values[0])
    for at in range(1, len(values)):
        if values[at] != values[at - 1]:
            result = jnp.where(index >= at, jnp.int32(values[at]), result)
    return result


def bit(mask, index):
    return jnp.bitwise_and(lax.shift_right_logical(jnp.int32(mask), index), 1)


def device(x, y, z, core):
    return (lax.div(x, 2) * 4 + y, lax.rem(x, 2) * 16 + z * 2 + core)


def kernel(
    owner, center, pair_occ, slab_map, eps_occ, eps_vir, eps_lines, vvvo, hole, amps, ints, out,
    mbuf, nbuf, obuf, acc, tiles, colabs, col, part, got1, got2,
    m_recv, m_send, z_recv, z_send, c_recv, c_send, local_sem, f_recv, f_send,
):
    grp, tile = lax.axis_index("grp"), lax.axis_index("tile")
    x_lo, z, core = lax.div(tile, 16), lax.div(lax.rem(tile, 16), 2), lax.rem(tile, 2)
    y, x = lax.rem(grp, 4), lax.div(grp, 4) * 2 + x_lo
    plane_pos, line_pos = x * 4 + y, z * 2 + core
    is_owner = grp == owner

    def plane_peer(n):
        pos = lax.rem(plane_pos + n, 16)
        return pos, device(lax.div(pos, 4), lax.rem(pos, 4), z, core)

    def line_peer(n):
        pos = lax.rem(line_pos + n, 16)
        return pos, device(x, y, lax.div(pos, 2), lax.rem(pos, 2))

    own_rows = pltpu.make_async_copy(vvvo, mbuf.at[:, x_lo, :, pl.ds(0, 1792)], local_sem.at[0])
    own_amps = pltpu.make_async_copy(
        amps, nbuf.at[0, pl.ds(pl.multiple_of(core * 112, 16), 112), pl.ds(0, 1792)], local_sem.at[1]
    )
    pl.when(is_owner)(own_rows.start)
    own_amps.start()

    barrier = pltpu.get_barrier_semaphore()
    for peer_of in (plane_peer, line_peer):
        for n in range(1, 16):
            pl.semaphore_signal(barrier, inc=1, device_id=peer_of(n)[1], device_id_type=MESH)

    zeros = jnp.zeros((112, 56), jnp.bfloat16)
    own_half = pl.ds(pl.multiple_of(core * 112, 16), 112)
    nbuf[0, own_half, 1792:2048] = jnp.concatenate([-ints[...], zeros], axis=1)

    @pl.when(is_owner)
    def _():
        for i in range(7):
            filled = jnp.concatenate([hole[i], jnp.zeros((128, 56), jnp.bfloat16)], axis=1)
            mbuf[i, x_lo, :, 1792:2048] = filled

    lane = lax.broadcasted_iota(jnp.int32, (8, 128), 1)
    flat = lax.broadcasted_iota(jnp.int32, (8, 128), 0) * 128 + lane
    slab = lax.shift_right_logical(flat * 1171, 16)
    within = flat - slab * 56
    slab_part = jnp.zeros((8, 128), jnp.float32)
    for a in range(16):
        slab_part = jnp.where(slab == a, eps_vir[slab_map[a]], slab_part)
    for s in range(2):
        tile_part = jnp.zeros((8, 128), jnp.float32)
        for r in range(56):
            tile_part = jnp.where(within == r, eps_vir[(s * 16 + z * 2 + core) * 56 + r], tile_part)
        outer = -(slab_part + tile_part)
        for i in range(7):
            line = jnp.broadcast_to(outer[i : i + 1, :], (128, 128))
            obuf[i, s * 128 : s * 128 + 128, :] = line.T
    occ = [eps_occ[center[0]] + eps_occ[pair_occ[p, 0]] + eps_occ[pair_occ[p, 1]] for p in range(2)]
    for n in range(16):
        first = (x_lo * 16 + n) * 56
        line, off = lax.div(first, 128), lax.rem(first, 128)
        both = [
            jnp.broadcast_to(eps_lines[pl.ds(lax.min(line + more, 13), 1), :], (8, 128)) for more in range(2)
        ]
        turned = [pltpu.roll(part_of, lax.rem(128 - off, 128), 1) for part_of in both]
        here = jnp.where(lane + off < 128, turned[0], turned[1])
        tiles[n % 2, n // 2 : n // 2 + 1, :] = here[0:1, :]
    even, odd = tiles[0], tiles[1]
    colabs[:, 0:128] = jnp.where(
        lane < 56,
        occ[0] - even,
        jnp.where(lane < 112, occ[1] - pltpu.roll(even, 56, 1), occ[0] - pltpu.roll(odd, 112, 1)),
    )
    colabs[:, 128:256] = jnp.where(
        lane < 40,
        occ[0] - pltpu.roll(odd, 112, 1),
        jnp.where(lane < 96, occ[1] - pltpu.roll(odd, 40, 1), -1.0),
    )
    for o in range(8):
        hops = (o + 1) // 2
        at = lax.rem(z + (8 - hops if o % 2 == 1 else hops), 8)
        col[o : o + 1, :] = colabs[pl.ds(at, 1), :]

    for slot in range(8):
        nbuf[slot, 224:256, :] = jnp.zeros((32, DEPTH), jnp.bfloat16)
    acc[...] = jnp.zeros_like(acc)
    part[...] = jnp.zeros_like(part)

    ahead = (device(x, y, lax.rem(z + 1, 8), core), device(x, y, lax.rem(z + 7, 8), core))
    sibling = device(x, y, z, 1 - core)
    piece = ((0, 64), (64, 48))

    def order_of(p, d):
        return 7 if d == 4 else (0 if d == 0 else 2 * d - 1 + p)

    def slot_rows(p, d, whose, c):
        first, size = (0, 112) if c is None else piece[c]
        return nbuf.at[order_of(p, d), pl.ds(pl.multiple_of(whose * 112 + first, 16), size)]

    def ring(p, d, c):
        return pltpu.make_async_remote_copy(
            slot_rows(p, d - 1, core, c), slot_rows(p, d, core, c), z_send.at[p, d - 1, c], z_recv.at[p, d - 1, c],
            device_id=ahead[p], device_id_type=MESH,
        )

    def share(p, d, c):
        here = slot_rows(p, d, core, c)
        sems = order_of(p, d), 0 if c is None else c
        return pltpu.make_async_remote_copy(
            here, here, c_send.at[sems], c_recv.at[sems], device_id=sibling, device_id_type=MESH
        )

    def shared(p, d, c):
        here = slot_rows(p, d, 1 - core, c)
        sems = order_of(p, d), 0 if c is None else c
        return pltpu.make_async_remote_copy(
            here, here, c_send.at[sems], c_recv.at[sems], device_id=sibling, device_id_type=MESH
        )

    def travels(p, d, c):
        return d <= 3 or (d == 4 and p == c)

    next_to = (
        device(lax.rem(x + 1, 4), y, z, core),
        device(lax.rem(x + 3, 4), y, z, core),
        device(x, lax.rem(y + 1, 4), z, core),
        device(x, lax.rem(y + 3, 4), z, core),
    )
    root_y, root_x = owner % 4, (owner // 4) * 2
    place = [lax.rem(x + 4 - root_x - s, 4) * 4 + lax.rem(y + 4 - root_y, 4) for s in range(2)]

    def of_core(table, j):
        return jnp.where(core == 0, jnp.int32(table[j]), jnp.int32(table[j + 2]))

    first_half = [
        [
            s + LAG * sum(bit(of_core([DEPTH_BITS[t][b] for t in range(4)], j), place[s]) * (1 << b) for b in range(3))
            for j in range(2)
        ]
        for s in range(2)
    ]
    child = [
        [[bit(of_core([CHILD_BITS[t][d] for t in range(4)], j), place[s]) == 1 for d in range(4)] for j in range(2)]
        for s in range(2)
    ]

    passes = [[child[s][j][0] | child[s][j][1] | child[s][j][2] | child[s][j][3] for j in range(2)] for s in range(2)]

    own_amps.wait()
    pl.semaphore_wait(barrier, 15 + 15)
    for c in range(2):
        for p in range(2):
            ring(p, 1, c).start()
    share(0, 0, None).start()
    pl.when(is_owner)(own_rows.wait)

    def row_events(half):
        for s in range(2):
            for j in range(2):
                since = half - first_half[s][j]

                @pl.when(passes[s][j] & (since >= 0) & (since < 2 * STEPS_ROWS) & (jnp.bitwise_and(since, 1) == 0))
                def _(s=s, j=j, since=since):
                    k = lax.shift_right_logical(since, 1)
                    q = since + j
                    part_rows = pl.ds(pl.multiple_of(lax.rem(q, BLOCK_CHUNKS) * CHUNK, CHUNK), CHUNK)
                    here = mbuf.at[lax.div(q, BLOCK_CHUNKS), s, part_rows]

                    def copy(d):
                        return pltpu.make_async_remote_copy(
                            here, here, m_send.at[s, j, d], m_recv.at[s, j, k],
                            device_id=next_to[d], device_id_type=MESH,
                        )

                    pl.when(place[s] != 0)(copy(0).wait_recv)
                    for d in range(4):
                        pl.when(child[s][j][d])(copy(d).start)

    def last_chunks(i):
        for s in range(2):
            for j in range(2):

                @pl.when(jnp.logical_not(passes[s][j]))
                def _(s=s, j=j):
                    for n in range(BLOCK_CHUNKS // 2):
                        here = mbuf.at[i, s, pl.ds((2 * n + j) * CHUNK, CHUNK)]
                        pltpu.make_async_remote_copy(
                            here, here, m_send.at[s, j, 0], m_recv.at[s, j, BLOCK_CHUNKS // 2 * i + n],
                            device_id=next_to[0], device_id_type=MESH,
                        ).wait_recv()

    def ring_event(n):
        d, c = (n // 2 + 1, n % 2) if n < 6 else (4, None)
        for p in range(2):
            cc = p if c is None else c
            ring(p, d, cc).wait_recv()
            if d < 4 and travels(p, d + 1, cc):
                ring(p, d + 1, cc).start()
            share(p, d, cc).start()

    def slots_shared(d):
        if d == 1:
            shared(0, 0, None).wait_recv()
        for p in range(2):
            for c in range(2):
                if travels(p, d, c):
                    shared(p, d, c).wait_recv()

    def unit(u, carry):
        word = pick(WORDS, lax.div(u, 6))
        code = jnp.bitwise_and(lax.shift_right_logical(word, 5 * lax.rem(u, 6)), 31)
        i, o = lax.div(code, 2), lax.rem(code, 2) * 4
        left = mbuf[i].reshape(256, DEPTH)
        right = nbuf[pl.ds(o, 4)].reshape(1024, DEPTH)
        w = lax.dot_general(left, right, (((1,), (1,)), ((), ())), preferred_element_type=jnp.float32)
        base = obuf[i]
        total = acc[i]
        for n in range(4):
            line = col[pl.ds(o + n, 1), :]
            for h in range(2):
                wh = w[:, 256 * n + 128 * h : 256 * n + 128 * h + 128]
                total = total + wh * wh / (base + line[:, 128 * h : 128 * h + 128])
        acc[i] = total

        @pl.when(o == 4)
        def _():
            for s in range(2):
                across = jnp.sum(total[128 * s : 128 * s + 128, :].T, axis=0, keepdims=True)
                part[s, pl.ds(i, 1), :] = across

        return carry

    def one_half(half, done):
        row_events(half)
        for n, when in enumerate(RING_STEPS):
            pl.when(half == when)(functools.partial(ring_event, n))
        for d in range(1, 5):
            pl.when(half == PAIR_READY[d - 1])(functools.partial(slots_shared, d))
        block = half - FIRST_BLOCK

        @pl.when((block >= 0) & (lax.rem(block, BLOCK_CHUNKS) == 0))
        def _():
            last_chunks(lax.div(block, BLOCK_CHUNKS))

        word = lax.div(half, 7)
        runs = jnp.bitwise_and(lax.shift_right_logical(pick(RUNS, word), 4 * (half - 7 * word)), 15)
        lax.fori_loop(done, done + runs, unit, 0)
        return done + runs

    lax.fori_loop(0, HALF_STEPS, one_half, jnp.int32(0))

    local = jnp.sum(part[0] + part[1], axis=0, keepdims=True)
    part[0, 7:8, :] = local
    part[1, 7:8, :] = local

    def exchange(stage, got, own_pos, peer_of, source):
        for n in range(1, 16):
            pos, peer = peer_of(n)
            pltpu.make_async_remote_copy(
                source(pos), got.at[own_pos], f_send.at[stage], f_recv.at[stage], device_id=peer, device_id_type=MESH
            ).start()

    def settle(stage, got, sems):
        whole = got.at[pl.ds(0, 15)]
        pltpu.make_async_copy(whole, whole, sems.at[stage]).wait()

    exchange(0, got1, plane_pos, plane_peer, lambda pos: part.at[lax.rem(lax.div(pos, 4), 2)])
    got1[plane_pos] = part[x_lo]

    for s in range(2):
        for j in range(2):
            for d in range(4):

                @pl.when(child[s][j][d])
                def _(s=s, j=j, d=d):
                    whole = mbuf.at[:, 0, pl.ds(0, STEPS_ROWS * CHUNK // 7)]
                    pltpu.make_async_copy(whole, whole, m_send.at[s, j, d]).wait()

    share(0, 0, None).wait_send()
    for d in range(1, 5):
        for p in range(2):
            for c in range(2):
                if travels(p, d, c):
                    ring(p, d, c).wait_send()
                    share(p, d, c).wait_send()

    settle(0, got1, f_recv)
    rows = got1[0]
    for n in range(1, 16):
        rows = rows + got1[n]
    got2[line_pos] = rows
    exchange(1, got2, line_pos, line_peer, lambda pos: got2.at[line_pos])
    out[0:8, :] = rows
    settle(0, got1, f_send)
    settle(1, got2, f_recv)
    every = got2[0]
    for n in range(1, 16):
        every = every + got2[n]
    out[8:16, :] = jnp.broadcast_to(jnp.sum(every[7:8, :], axis=1, keepdims=True), (8, 128))
    settle(1, got2, f_send)


def triples(owner, *operands):
    bf16, f32 = jnp.bfloat16, jnp.float32
    smem, vmem = pl.BlockSpec(memory_space=pltpu.SMEM), pl.BlockSpec(memory_space=pltpu.VMEM)
    anywhere = pl.BlockSpec(memory_space=pl.ANY)
    return pl.pallas_call(
        functools.partial(kernel, owner),
        out_shape=jax.ShapeDtypeStruct((16, 128), f32),
        in_specs=[smem, smem, smem, smem, smem, vmem, anywhere, vmem, anywhere, vmem],
        out_specs=vmem,
        scratch_shapes=[
            pltpu.VMEM((7, 2, 128, DEPTH), bf16),
            pltpu.VMEM((8, 256, DEPTH), bf16),
            pltpu.VMEM((7, 256, 128), f32),
            pltpu.VMEM((7, 256, 128), f32),
            pltpu.VMEM((2, 8, 128), f32),
            pltpu.VMEM((8, 256), f32),
            pltpu.VMEM((8, 256), f32),
            pltpu.VMEM((2, 8, 128), f32),
            pltpu.VMEM((16, 8, 128), f32),
            pltpu.VMEM((16, 8, 128), f32),
            pltpu.SemaphoreType.DMA((2, 2, STEPS_ROWS)),
            pltpu.SemaphoreType.DMA((2, 2, 4)),
            pltpu.SemaphoreType.DMA((2, 4, 2)),
            pltpu.SemaphoreType.DMA((2, 4, 2)),
            pltpu.SemaphoreType.DMA((8, 2)),
            pltpu.SemaphoreType.DMA((8, 2)),
            pltpu.SemaphoreType.DMA((2,)),
            pltpu.SemaphoreType.DMA((2,)),
            pltpu.SemaphoreType.DMA((2,)),
        ],
        compiler_params=pltpu.CompilerParams(
            collective_id=owner, has_side_effects=True, vmem_limit_bytes=48 << 20
        ),
        name="triples",
    )(*operands)


def shards(center, pair_occ, slab_map, eps_occ, eps_vir, vvvo, hole_amps, pair_amps, pair_ints):
    operands = (
        center,
        pair_occ,
        slab_map,
        eps_occ,
        eps_vir,
        eps_vir.reshape(14, 128),
        vvvo.reshape(7, 128, 1792),
        hole_amps.reshape(7, 128, 200),
        pair_amps.reshape(112, 1792),
        pair_ints.reshape(112, 200),
    )
    out = lax.switch(center[0], [functools.partial(triples, n) for n in range(8)], *operands)
    return out[0:7].reshape(16, 56), out[8, 0]


def solution(mesh):
    in_specs = (
        P(),
        P("grp", None),
        P(),
        P(),
        P(),
        P("grp", None, "tile", None),
        P("grp", None, "tile", None),
        P("grp", "tile", None),
        P("grp", "tile", None),
    )
    out_specs = (P(None, "tile"), P())
    return jax.shard_map(shards, mesh=mesh, in_specs=in_specs, out_specs=out_specs, check_vma=False)
```
